32 devices in a mesh: groups: 2 (over y), wide: 4 (over z), narrow: 4 (over x, core).
Axes of the slice: x: 2, y: 2, z: 4, core: 2. Of those that a mesh axis runs over, the one named last changes fastest.
Arguments:
- cand_acts: bfloat16 [2048, 28672], P(('groups', 'narrow'), 'wide'), parts along dimension 0, may hold values from -6 to 6
- cand_grads: bfloat16 [2048, 8192], P(('groups', 'narrow'), 'wide'), parts along dimension 0, may hold values from -6 to 6
- query_acts: bfloat16 [512, 28672], P('groups', 'wide'), parts along dimension 0, may hold values from -6 to 6
- query_grads: bfloat16 [512, 8192], P('groups', 'wide'), parts along dimension 0, may hold values from -6 to 6
- basis_in: bfloat16 [28672, 512], P('wide'), may hold values from -0.03125 to 0.03125
- basis_out: bfloat16 [8192, 256], P('wide'), may hold values from -0.0625 to 0.0625
- eigvals: float32 [256, 512], P(None, 'wide'), may hold values from 0.25 to 4
- slot_pair: int32 [2048], P(('groups', 'narrow')), parts along dimension 0, may hold values from 0 to 128, as said below
Outputs:
- scores: float32 [256, 64], P(('groups', 'wide', 'narrow')), parts along dimension 0
The draws below stay inside these ranges and needn't reach their ends.
There are 2 independent parts, one for each index of `groups`. The reference program is written for one: setup_inputs(seed, part) draws one part's arguments, and reference() takes and returns one part's arrays. A program takes and returns all parts, laid end to end along the dimension named above; an argument that names none is the same for every part. Nothing has to cross between parts.
Inputs may be any that keep to these rules, and one draw needn't show every extreme that they name: `slot_pair`: on each index of narrow the live slots (value below 128) come first among its 256 slots and the others hold 128. Live slots over all devices number exactly 512; read in device order their values never fall and every pair has one or more. In every draw the slots of some index of narrow are all live.
All inputs are finite; a program needn't handle non-finite values.
Results may differ from the reference program's by a relative error of at most 0.004.
Values may be sent and summed in bfloat16 or wider, within the bound.
A program may use at most 64 MiB of HBM per device.

```python
import math
import jax
import jax.numpy as jnp
from jax import lax

D = 8192
FFN = 28672
KA_DEV = 128
KG = 256
QUERIES = 64
QPER = 4
TOK_DEV = 128
PAIRS = 128
KA = 512
SLOTS = 256
TOKENS = 512
QTOK = 256
N_WIDE = 4
N_NARROW = 4


def draw_slot_pair(key, part):
    key = jax.random.fold_in(key, 7)
    key_heavy, key_delta, key_cuts = jax.random.split(key, 3)
    slot_count = 2 * TOK_DEV
    total = TOK_DEV * N_NARROW
    others = N_NARROW - 1
    rest = total - slot_count
    base_load = rest // others
    spread = base_load // (2 * others)
    deltas = jax.random.randint(key_delta, (others,), -spread, spread + 1)
    deltas = deltas.at[others - 1].set(0)
    deltas = deltas.at[others - 1].set(-jnp.sum(deltas))
    loads = base_load + deltas
    loads = loads.at[others - 1].add(rest - base_load * others)
    heavy_dev = jax.random.randint(key_heavy, (), 0, N_NARROW)
    device_ids = jnp.arange(N_NARROW)
    other_slot = jnp.clip(device_ids - (device_ids > heavy_dev).astype(jnp.int32), 0, others - 1)
    counts = jnp.where(device_ids == heavy_dev, slot_count, loads[other_slot])
    starts = jnp.cumsum(counts) - counts
    cut_points = jax.random.permutation(key_cuts, total - 1)[:PAIRS - 1] + 1
    flags = jnp.zeros((total,), jnp.int32).at[cut_points].set(1)
    pair_of = jnp.cumsum(flags)
    slot_ids = jnp.arange(slot_count)
    position = starts[:, None] + slot_ids[None, :]
    is_live = slot_ids[None, :] < counts[:, None]
    values = jnp.where(is_live, pair_of[jnp.clip(position, 0, total - 1)], PAIRS)
    return values.reshape(-1).astype(jnp.int32)


def steps_of(stream_key, extent, shards, low, high):
    factor_of = 1.0
    for dim, parts in shards:
        heights = jax.random.uniform(jax.random.fold_in(jax.random.fold_in(stream_key, 6), dim), (parts,), jnp.float32, low / len(shards), high / len(shards))
        factor_of = factor_of * jnp.repeat(jnp.exp(heights), extent[dim] // parts).reshape((-1,) + (1,) * (len(extent) - 1 - dim))
    return factor_of


def bell_draw(key, extent, width, limit, cuts=(), kind=jnp.bfloat16):
    array = width * jax.random.normal(key, extent, jnp.float32)
    if cuts:
        array = array * steps_of(key, extent, cuts, -0.22, 0.18)
    return jnp.clip(array, -limit, limit).astype(kind)


def setup_inputs(seed: int = 0, part: int = 0) -> dict:
    key_of = jax.random.split(jax.random.key(seed), 9)
    part_splits = jax.random.split(jax.random.fold_in(key_of[8], part), 9)
    return {
        "cand_acts": bell_draw(part_splits[0], (SLOTS * N_NARROW, FFN), 1.0, 6.0, ((0, 4), (1, 4))),
        "cand_grads": bell_draw(part_splits[1], (SLOTS * N_NARROW, D), 1.0, 6.0, ((0, 4), (1, 4))),
        "query_acts": bell_draw(part_splits[2], (QTOK, FFN), 1.0, 6.0, ((1, 4),)),
        "query_grads": bell_draw(part_splits[3], (QTOK, D), 1.0, 6.0, ((1, 4),)),
        "basis_in": bell_draw(key_of[4], (FFN, KA), FFN ** -0.5, 0.03125, ((0, 4),)),
        "basis_out": bell_draw(key_of[5], (D, KG), D ** -0.5, 0.0625, ((0, 4),)),
        "eigvals": jnp.clip(jnp.exp(math.log(4.0) - 2.7725887 * jax.random.uniform(key_of[6], (KG, KA), jnp.float32) ** steps_of(key_of[6], (KG, KA), ((1, 4),), -0.2, 0.2)), 0.25, 4.0),
        "slot_pair": draw_slot_pair(jax.random.fold_in(jax.random.fold_in(key_of[8], part), 71), part),
    }


def reference(cand_acts, cand_grads, query_acts, query_grads, basis_in, basis_out, eigvals, slot_pair):
    live_rows = jnp.nonzero(slot_pair < PAIRS, size=TOKENS)[0].astype(jnp.int32)
    live_acts = jnp.take(cand_acts, live_rows, axis=0)
    live_grads = jnp.take(cand_grads, live_rows, axis=0)
    live_pairs = jnp.take(slot_pair, live_rows, axis=0)
    act_proj = jnp.dot(live_acts, basis_in, preferred_element_type=jnp.float32)
    grad_proj = jnp.dot(live_grads, basis_out, preferred_element_type=jnp.float32).astype(jnp.bfloat16)
    query_proj = jnp.dot(query_acts, basis_in, preferred_element_type=jnp.float32)
    query_out = jnp.dot(query_grads, basis_out, preferred_element_type=jnp.float32)
    kept_total = KA_DEV * N_WIDE
    ratio_table = jnp.einsum('qpi,qpj->iqj', query_out.reshape(QUERIES, QPER, KG), query_proj.reshape(QUERIES, QPER, kept_total), precision=lax.Precision.HIGHEST) / eigvals[:, None, :]
    ratio_table = ratio_table.astype(jnp.bfloat16).reshape(KG, QUERIES * kept_total)
    block_rows = math.gcd(TOKENS, 64)
    block_count = TOKENS // block_rows

    def score_block(pieces):
        grad_block, act_block = pieces
        product = jnp.dot(grad_block, ratio_table, preferred_element_type=jnp.float32)
        product = product.reshape(block_rows, QUERIES, kept_total)
        return jnp.einsum('bqj,bj->bq', product, act_block, precision=lax.Precision.HIGHEST)
    token_scores = lax.map(score_block, (grad_proj.reshape(block_count, block_rows, KG), act_proj.reshape(block_count, block_rows, kept_total)))
    token_scores = token_scores.reshape(TOKENS, QUERIES)
    onehot = (live_pairs[None, :] == jnp.arange(PAIRS, dtype=jnp.int32)[:, None]).astype(jnp.float32)
    totals = jnp.dot(onehot, token_scores, precision=lax.Precision.HIGHEST)
    score_scale = 1.0 / math.sqrt(KG * KA_DEV * N_WIDE * QPER * TOK_DEV * N_NARROW / PAIRS)
    return totals * score_scale
```

```python
import functools
import math

import jax
import jax.numpy as jnp
from jax import lax
from jax.experimental import pallas as pl
from jax.experimental.pallas import tpu as pltpu
from jax.sharding import PartitionSpec as P

QPER = 4
TOK_DEV = 128
PAIRS = 128
MESH = pl.DeviceIdType.MESH
F32 = jnp.float32
BF16 = jnp.bfloat16


def nt_dot(a, b, precision=None):
    return lax.dot_general(
        a, b, (((1,), (1,)), ((), ())), precision=precision, preferred_element_type=F32
    )


def tn_dot(a, b):
    return lax.dot_general(a, b, (((0,), (0,)), ((), ())), preferred_element_type=F32)


def kernel(
    W, N, scale,
    ca, cg, qa, qg, bi, bo, eig, sp,
    out,
    x, vbi, vcg, vqg, vbo, acc,
    g_own, g_send, g_recv, g_all,
    o_send, o_recv, o_all,
    p_send, p_recv, a_send, a_recv,
    qo_all, qp_all,
    qp3, qo3, table, act_t, grad, tsc,
    f_send, f_recv,
    ld_sem, bi_sem, ca_sem, qa_sem,
    gs_s, gs_r, ga_s, ga_r, os_s, os_r, oa_s, oa_r,
    ps_s, ps_r, as_s, as_r, no_s, no_r, np_s, np_r, f_s, f_r,
):
    w = lax.axis_index("wide")
    n = lax.axis_index("narrow")
    me = w * N + n
    C, rows, CK = x.shape
    T = ca.shape[0]
    QN = rows - T
    G = bo.shape[1]
    J = eig.shape[1]
    TW = g_send.shape[1]
    QW = o_send.shape[1]
    PR = f_send.shape[1]
    queries = N * QN // QPER
    wire = g_send.dtype

    q_rows = pl.ds(pl.multiple_of(n * QN, QN), QN)
    loads = [
        pltpu.make_async_copy(bo, vbo, ld_sem.at[0]),
        pltpu.make_async_copy(cg, vcg, ld_sem.at[1]),
        pltpu.make_async_copy(qg.at[q_rows], vqg, ld_sem.at[2]),
    ]
    for c in loads:
        c.start()

    def chunk_copies(c):
        cols = pl.ds(c * CK, CK)
        return (
            pltpu.make_async_copy(bi.at[cols], vbi.at[c], bi_sem.at[c]),
            pltpu.make_async_copy(ca.at[:, cols], x.at[c, pl.ds(0, T)], ca_sem.at[c]),
            pltpu.make_async_copy(qa.at[q_rows, cols], x.at[c, pl.ds(T, QN)], qa_sem.at[c]),
        )

    for c in range(C):
        for copy in chunk_copies(c):
            copy.start()

    barrier = pltpu.get_barrier_semaphore()

    def greet(d, _):
        k = lax.rem(me + d, W * N)
        pl.semaphore_signal(
            barrier, inc=1, device_id={"wide": k // N, "narrow": lax.rem(k, N)},
            device_id_type=MESH,
        )
        return 0

    lax.fori_loop(1, W * N, greet, 0)

    def wide_of(d):
        return lax.rem(w + d, W)

    def scatter(send, recv, s, r, d):
        k = wide_of(d)
        return pltpu.make_async_remote_copy(
            src_ref=send.at[k], dst_ref=recv.at[d], send_sem=s.at[d], recv_sem=r.at[d],
            device_id={"wide": k}, device_id_type=MESH,
        )

    def gather(buf, s, r, d):
        return pltpu.make_async_remote_copy(
            src_ref=buf.at[w], dst_ref=buf.at[w], send_sem=s.at[d], recv_sem=r.at[d],
            device_id={"wide": wide_of(d)}, device_id_type=MESH,
        )

    def share(buf, s, r, d):
        return pltpu.make_async_remote_copy(
            src_ref=buf.at[n], dst_ref=buf.at[n], send_sem=s.at[d], recv_sem=r.at[d],
            device_id={"narrow": lax.rem(n + d, N)}, device_id_type=MESH,
        )

    def final(d):
        k = lax.rem(me + d, W * N)
        return pltpu.make_async_remote_copy(
            src_ref=f_send.at[k], dst_ref=f_recv.at[d], send_sem=f_s.at[d], recv_sem=f_r.at[d],
            device_id={"wide": k // N, "narrow": lax.rem(k, N)}, device_id_type=MESH,
        )

    def each(count, make, what):
        def body(d, _):
            getattr(make(d), what)()
            return 0

        lax.fori_loop(1, count, body, 0)

    grad_rs = functools.partial(scatter, g_send, g_recv, gs_s, gs_r)
    out_rs = functools.partial(scatter, o_send, o_recv, os_s, os_r)
    proj_rs = functools.partial(scatter, p_send, p_recv, ps_s, ps_r)
    act_rs = functools.partial(scatter, a_send, a_recv, as_s, as_r)
    grad_ag = functools.partial(gather, g_all, ga_s, ga_r)
    out_ag = functools.partial(gather, o_all, oa_s, oa_r)
    out_sh = functools.partial(share, qo_all, no_s, no_r)
    proj_sh = functools.partial(share, qp_all, np_s, np_r)

    for c in loads:
        c.wait()
    part = jnp.dot(vcg[...], vbo[...], preferred_element_type=F32)
    for k in range(W):
        block = part[k * TW : (k + 1) * TW]
        g_own[k] = block
        g_send[k] = block.astype(wire)
    part = jnp.dot(vqg[...], vbo[...], preferred_element_type=F32)
    for k in range(W):
        o_send[k] = part[k * QW : (k + 1) * QW]

    pl.semaphore_wait(barrier, W * N - 1)
    each(W, out_rs, "start")
    each(W, grad_rs, "start")

    def project(c, _):
        cols = pl.ds(c * CK, CK)
        pltpu.make_async_copy(bi.at[cols], vbi.at[c], bi_sem.at[c]).wait()
        pltpu.make_async_copy(ca.at[:, cols], x.at[c, pl.ds(0, T)], ca_sem.at[c]).wait()
        pltpu.make_async_copy(
            qa.at[q_rows, cols], x.at[c, pl.ds(T, QN)], qa_sem.at[c]
        ).wait()
        acc[...] += jnp.dot(x[c], vbi[c], preferred_element_type=F32)
        return 0

    acc[...] = jnp.zeros_like(acc)
    mid = max(C - 2, 0)
    lax.fori_loop(0, mid, project, 0)

    each(W, out_rs, "wait_recv")
    total = o_send[w]
    for d in range(1, W):
        total = total + o_recv[d]
    o_all[w] = total
    each(W, out_ag, "start")
    each(W, grad_rs, "wait_recv")
    total = g_own[w]
    for d in range(1, W):
        total = total + g_recv[d].astype(F32)
    g_all[w] = total.astype(BF16).astype(wire)
    each(W, grad_ag, "start")

    lax.fori_loop(mid, C, project, 0)

    for k in range(W):
        p_send[k] = acc[T:, k * J : (k + 1) * J]
    each(W, proj_rs, "start")
    for k in range(W):
        a_send[k] = acc[:T, k * J : (k + 1) * J].astype(BF16)
    each(W, act_rs, "start")

    recip = (1.0 / eig[...]).T
    each(W, out_ag, "wait_recv")
    for k in range(W):
        qo_all[n, k * QW : (k + 1) * QW, :] = o_all[k]
    each(N, out_sh, "start")
    each(W, proj_rs, "wait_recv")
    total = p_send[w]
    for d in range(1, W):
        total = total + p_recv[d]
    qp_all[n] = total
    each(N, proj_sh, "start")

    each(N, out_sh, "wait_recv")
    groups, three, _ = qp3.shape
    GT = three // 3
    per = QN // GT
    for g in range(groups):
        at, lo = g // per, (g % per) * GT
        val = qo_all[at, lo : lo + GT, :]
        hi = val.astype(BF16)
        low = (val - hi.astype(F32)).astype(BF16)
        qo3[g, 0:GT] = hi
        qo3[g, GT : 2 * GT] = low
        qo3[g, 2 * GT :] = hi
    each(N, proj_sh, "wait_recv")
    for g in range(groups):
        at, lo = g // per, (g % per) * GT
        val = qp_all[at, lo : lo + GT, :]
        hi = val.astype(BF16)
        low = (val - hi.astype(F32)).astype(BF16)
        qp3[g, 0:GT] = hi
        qp3[g, GT : 2 * GT] = hi
        qp3[g, 2 * GT :] = low

    GQ = GT // QPER
    token = lax.rem(lax.broadcasted_iota(jnp.int32, (three, G), 0), GT)

    def build(g, _):
        left = qp3[g]
        right = qo3[g].astype(F32)
        for k in range(GQ):
            mine = jnp.where((token >= k * QPER) & (token < (k + 1) * QPER), right, 0.0)
            block = tn_dot(left, mine.astype(BF16)) * recip
            table[g, k * J : (k + 1) * J, :] = block.astype(BF16)
        return 0

    lax.fori_loop(0, groups, build, 0)

    each(W, grad_ag, "wait_recv")
    for k in range(W):
        grad[k * TW : (k + 1) * TW, :] = g_all[k].astype(F32)
    grads = grad[...].astype(BF16)
    tsc[...] = jnp.zeros_like(tsc)
    each(W, act_rs, "wait_recv")
    own = a_send[w].astype(F32)
    for d in range(1, W):
        own = own + a_recv[d].astype(F32)
    act_t[...] = own.T

    def score(g, _):
        h = nt_dot(table[g], grads)
        for k in range(GQ):
            rowsum = jnp.sum(h[k * J : (k + 1) * J] * act_t[...], axis=0, keepdims=True)
            tsc[pl.ds(g * GQ + k, 1), :] = rowsum
        return 0

    lax.fori_loop(0, groups, score, 0)

    pair = lax.broadcasted_iota(jnp.int32, (PAIRS, T), 0)
    onehot = (pair == sp[...]).astype(F32)
    value = nt_dot(onehot, tsc[...], lax.Precision.HIGHEST)
    for k in range(W * N):
        f_send[k] = value[k * PR : (k + 1) * PR]
    each(W * N, final, "start")
    each(W * N, final, "wait_recv")
    total = f_send[me]
    for d in range(1, W * N):
        total = total + f_recv[d]
    out[...] = total[:, :queries] * scale

    for count, make in (
        (W, out_rs), (W, grad_rs), (W, out_ag), (W, grad_ag), (W, proj_rs), (W, act_rs),
        (N, out_sh), (N, proj_sh), (W * N, final),
    ):
        each(count, make, "wait_send")


def per_device(
    cand_acts, cand_grads, query_acts, query_grads, basis_in, basis_out, eigvals, slot_pair
):
    W = lax.axis_size("wide")
    N = lax.axis_size("narrow")
    T, F = cand_acts.shape
    D = cand_grads.shape[1]
    Q = query_acts.shape[0]
    KA = basis_in.shape[1]
    G, J = eigvals.shape
    QN = Q // N
    TW, QW = T // W, QN // W
    PR = PAIRS // (W * N)
    queries = Q // QPER
    qpad = -(-queries // 128) * 128
    C = next(c for c in range(max(F // 1024, 1), F + 1) if F % (c * 128) == 0)
    CK = F // C
    GT = 32
    groups = Q // GT
    wire = BF16 if TW % 16 == 0 else F32
    scale = 1.0 / math.sqrt(G * J * W * QPER * TOK_DEV * N / PAIRS)
    vm = pltpu.VMEM
    dma = pltpu.SemaphoreType.DMA
    scratch = [
        vm((C, T + QN, CK), BF16), vm((C, CK, KA), BF16), vm((T, D), BF16), vm((QN, D), BF16),
        vm((D, G), BF16), vm((T + QN, KA), F32),
        vm((W, TW, G), F32), vm((W, TW, G), wire), vm((W, TW, G), wire), vm((W, TW, G), wire),
        vm((W, QW, G), F32), vm((W, QW, G), F32), vm((W, QW, G), F32),
        vm((W, QN, J), F32), vm((W, QN, J), F32), vm((W, T, J), BF16), vm((W, T, J), BF16),
        vm((N, QN, G), F32), vm((N, QN, J), F32),
        vm((groups, 3 * GT, J), BF16), vm((groups, 3 * GT, G), BF16),
        vm((groups, GT // QPER * J, G), BF16), vm((J, T), F32), vm((T, G), F32), vm((qpad, T), F32),
        vm((W * N, PR, qpad), F32), vm((W * N, PR, qpad), F32),
        dma((3,)), dma((C,)), dma((C,)), dma((C,)),
    ] + [dma((W,))] * 12 + [dma((N,))] * 4 + [dma((W * N,))] * 2
    hbm = pl.BlockSpec(memory_space=pl.ANY)
    vmem = pl.BlockSpec(memory_space=pltpu.VMEM)
    return pl.pallas_call(
        functools.partial(kernel, W, N, scale),
        out_shape=jax.ShapeDtypeStruct((PR, queries), F32),
        in_specs=[hbm] * 6 + [vmem] * 2,
        out_specs=vmem,
        scratch_shapes=scratch,
        compiler_params=pltpu.CompilerParams(
            collective_id=0, has_side_effects=True, vmem_limit_bytes=50 * 2**20
        ),
        cost_estimate=pl.CostEstimate(
            flops=2 * (T + QN) * F * KA, bytes_accessed=2 * F * (KA + T + QN), transcendentals=0
        ),
    )(
        cand_acts, cand_grads, query_acts, query_grads, basis_in, basis_out, eigvals,
        slot_pair.reshape(1, T),
    )


def solution(mesh):
    in_specs = (
        P(("groups", "narrow"), "wide"),
        P(("groups", "narrow"), "wide"),
        P("groups", "wide"),
        P("groups", "wide"),
        P("wide", None),
        P("wide", None),
        P(None, "wide"),
        P(("groups", "narrow")),
    )
    out_specs = P(("groups", "wide", "narrow"), None)
    return jax.shard_map(
        per_device, mesh=mesh, in_specs=in_specs, out_specs=out_specs, check_vma=False
    )
```

```python
import functools
import math

import jax
import jax.numpy as jnp
from jax import lax
from jax.experimental import pallas as pl
from jax.experimental.pallas import tpu as pltpu
from jax.sharding import PartitionSpec as P

QPER = 4
TOK_DEV = 128
PAIRS = 128
MESH = pl.DeviceIdType.MESH
F32 = jnp.float32
BF16 = jnp.bfloat16


def nt_dot(a, b, precision=None):
    return lax.dot_general(
        a, b, (((1,), (1,)), ((), ())), precision=precision, preferred_element_type=F32
    )


def tn_dot(a, b):
    return lax.dot_general(a, b, (((0,), (0,)), ((), ())), preferred_element_type=F32)


def kernel(
    W, N, scale,
    ca, cg, qa, qg, bi, bo, eig_hbm, sp_hbm,
    out,
    eig, sp, x, vbi, vcg, vqg, vbo, acc,
    g_own, g_send, g_recv, g_all,
    o_send, o_recv, o_all,
    p_send, p_recv, a_send, a_recv,
    qo_all, qp_all,
    table, act_t, grad, tsc,
    f_send, f_recv,
    ld_sem, bi_sem, ca_sem, qa_sem,
    gs_s, gs_r, ga_s, ga_r, os_s, os_r, oa_s, oa_r,
    ps_s, ps_r, as_s, as_r, no_s, no_r, np_s, np_r, f_s, f_r,
):
    w = lax.axis_index("wide")
    n = lax.axis_index("narrow")
    me = w * N + n
    C, rows, CK = x.shape
    T = ca.shape[0]
    QN = rows - T
    G = bo.shape[1]
    J = eig.shape[1]
    TW = g_send.shape[1]
    QW = o_send.shape[1]
    PR = f_send.shape[1]
    queries = N * QN // QPER
    wire = g_send.dtype

    q_rows = pl.ds(pl.multiple_of(n * QN, QN), QN)
    loads = [
        pltpu.make_async_copy(bo, vbo, ld_sem.at[0]),
        pltpu.make_async_copy(qg.at[q_rows], vqg, ld_sem.at[1]),
        pltpu.make_async_copy(cg, vcg, ld_sem.at[2]),
    ]
    late = [
        pltpu.make_async_copy(eig_hbm, eig, ld_sem.at[3]),
        pltpu.make_async_copy(sp_hbm, sp, ld_sem.at[4]),
    ]
    for c in loads:
        c.start()

    def chunk_copies(c):
        cols = pl.ds(c * CK, CK)
        return (
            pltpu.make_async_copy(bi.at[cols], vbi.at[c], bi_sem.at[c]),
            pltpu.make_async_copy(ca.at[:, cols], x.at[c, pl.ds(0, T)], ca_sem.at[c]),
            pltpu.make_async_copy(qa.at[q_rows, cols], x.at[c, pl.ds(T, QN)], qa_sem.at[c]),
        )

    for c in range(C):
        for copy in chunk_copies(c):
            copy.start()
    for c in late:
        c.start()

    barrier = pltpu.get_barrier_semaphore()

    def greet(d, _):
        k = lax.rem(me + d, W * N)
        pl.semaphore_signal(
            barrier, inc=1, device_id={"wide": k // N, "narrow": lax.rem(k, N)},
            device_id_type=MESH,
        )
        return 0

    lax.fori_loop(1, W * N, greet, 0)

    def wide_of(d):
        return lax.rem(w + d, W)

    def scatter(send, recv, s, r, d):
        k = wide_of(d)
        return pltpu.make_async_remote_copy(
            src_ref=send.at[k], dst_ref=recv.at[d], send_sem=s.at[d], recv_sem=r.at[d],
            device_id={"wide": k}, device_id_type=MESH,
        )

    def gather(buf, s, r, d):
        return pltpu.make_async_remote_copy(
            src_ref=buf.at[w], dst_ref=buf.at[w], send_sem=s.at[d], recv_sem=r.at[d],
            device_id={"wide": wide_of(d)}, device_id_type=MESH,
        )

    def share(buf, s, r, d):
        return pltpu.make_async_remote_copy(
            src_ref=buf.at[n], dst_ref=buf.at[n], send_sem=s.at[d], recv_sem=r.at[d],
            device_id={"narrow": lax.rem(n + d, N)}, device_id_type=MESH,
        )

    def final(d):
        k = lax.rem(me + d, W * N)
        return pltpu.make_async_remote_copy(
            src_ref=f_send.at[k], dst_ref=f_recv.at[d], send_sem=f_s.at[d], recv_sem=f_r.at[d],
            device_id={"wide": k // N, "narrow": lax.rem(k, N)}, device_id_type=MESH,
        )

    def each(count, make, what):
        def body(d, _):
            getattr(make(d), what)()
            return 0

        lax.fori_loop(1, count, body, 0)

    grad_rs = functools.partial(scatter, g_send, g_recv, gs_s, gs_r)
    out_rs = functools.partial(scatter, o_send, o_recv, os_s, os_r)
    proj_rs = functools.partial(scatter, p_send, p_recv, ps_s, ps_r)
    act_rs = functools.partial(scatter, a_send, a_recv, as_s, as_r)
    grad_ag = functools.partial(gather, g_all, ga_s, ga_r)
    out_ag = functools.partial(gather, o_all, oa_s, oa_r)
    out_sh = functools.partial(share, qo_all, no_s, no_r)
    proj_sh = functools.partial(share, qp_all, np_s, np_r)

    loads[0].wait()
    loads[1].wait()
    part = jnp.dot(vqg[...], vbo[...], preferred_element_type=F32)
    for k in range(W):
        o_send[k] = part[k * QW : (k + 1) * QW]
    loads[2].wait()
    part = jnp.dot(vcg[...], vbo[...], preferred_element_type=F32)
    for k in range(W):
        block = part[k * TW : (k + 1) * TW]
        g_own[k] = block
        g_send[k] = block.astype(wire)

    def project(c, _):
        cols = pl.ds(c * CK, CK)
        pltpu.make_async_copy(bi.at[cols], vbi.at[c], bi_sem.at[c]).wait()
        pltpu.make_async_copy(ca.at[:, cols], x.at[c, pl.ds(0, T)], ca_sem.at[c]).wait()
        pltpu.make_async_copy(
            qa.at[q_rows, cols], x.at[c, pl.ds(T, QN)], qa_sem.at[c]
        ).wait()
        acc[...] += jnp.dot(x[c], vbi[c], preferred_element_type=F32)
        return 0

    acc[...] = jnp.zeros_like(acc)
    first, mid = C * 2 // 7, C * 5 // 7
    lax.fori_loop(0, first, project, 0)
    pl.semaphore_wait(barrier, W * N - 1)
    each(W, out_rs, "start")
    each(W, grad_rs, "start")
    lax.fori_loop(first, mid, project, 0)

    each(W, out_rs, "wait_recv")
    total = o_send[w]
    for d in range(1, W):
        total = total + o_recv[d]
    o_all[w] = total
    each(W, out_ag, "start")
    lax.fori_loop(mid, C, project, 0)

    for k in range(W):
        p_send[k] = acc[T:, k * J : (k + 1) * J]
    each(W, proj_rs, "start")

    each(W, out_ag, "wait_recv")
    for k in range(W):
        qo_all[n, k * QW : (k + 1) * QW, :] = o_all[k]
    each(N, out_sh, "start")

    each(W, grad_rs, "wait_recv")
    total = g_own[w]
    for d in range(1, W):
        total = total + g_recv[d].astype(F32)
    g_all[w] = total.astype(BF16).astype(wire)
    each(W, grad_ag, "start")
    for k in range(W):
        a_send[k] = acc[:T, k * J : (k + 1) * J].astype(BF16)
    each(W, act_rs, "start")

    for c in late:
        c.wait()
    recip = (1.0 / eig[...]).T
    each(W, proj_rs, "wait_recv")
    total = p_send[w]
    for d in range(1, W):
        total = total + p_recv[d]
    qp_all[n] = total
    each(N, proj_sh, "start")

    groups, GT = table.shape[0], table.shape[1] // J * QPER
    three = 3 * GT
    per = QN // GT
    GQ = GT // QPER
    token = lax.rem(lax.broadcasted_iota(jnp.int32, (three, G), 0), GT)

    def build(step, _):
        d = step // per

        @pl.when((d > 0) & (lax.rem(step, per) == 0))
        def _():
            out_sh(d).wait_recv()
            proj_sh(d).wait_recv()

        at = lax.rem(n + N - d, N)
        lo = pl.multiple_of(lax.rem(step, per) * GT, GT)
        val = qp_all[at, pl.ds(lo, GT), :]
        hi = val.astype(BF16).astype(F32)
        left = jnp.concatenate([hi, hi, val - hi], axis=0).astype(BF16)
        val = qo_all[at, pl.ds(lo, GT), :]
        hi = val.astype(BF16).astype(F32)
        right = jnp.concatenate([hi, val - hi, hi], axis=0)
        g = at * per + lax.rem(step, per)
        for k in range(GQ):
            mine = jnp.where((token >= k * QPER) & (token < (k + 1) * QPER), right, 0.0)
            block = tn_dot(left, mine.astype(BF16)) * recip
            table[g, k * J : (k + 1) * J, :] = block.astype(BF16)
        return 0

    lax.fori_loop(0, groups, build, 0)

    each(W, grad_ag, "wait_recv")
    for k in range(W):
        grad[k * TW : (k + 1) * TW, :] = g_all[k].astype(F32)
    grads = grad[...].astype(BF16)
    tsc[...] = jnp.zeros_like(tsc)
    each(W, act_rs, "wait_recv")
    own = a_send[w].astype(F32)
    for d in range(1, W):
        own = own + a_recv[d].astype(F32)
    act_t[...] = own.T

    def score(g, _):
        h = nt_dot(table[g], grads)
        for k in range(GQ):
            rowsum = jnp.sum(h[k * J : (k + 1) * J] * act_t[...], axis=0, keepdims=True)
            tsc[pl.ds(g * GQ + k, 1), :] = rowsum
        return 0

    lax.fori_loop(0, groups, score, 0)

    pair = lax.broadcasted_iota(jnp.int32, (PAIRS, T), 0)
    onehot = (pair == sp[...]).astype(F32)
    value = nt_dot(onehot, tsc[...], lax.Precision.HIGHEST)
    for k in range(W * N):
        f_send[k] = value[k * PR : (k + 1) * PR]
    each(W * N, final, "start")
    each(W * N, final, "wait_recv")
    total = f_send[me]
    for d in range(1, W * N):
        total = total + f_recv[d]
    out[...] = total[:, :queries] * scale

    for count, make in (
        (W, out_rs), (W, grad_rs), (W, out_ag), (W, grad_ag), (W, proj_rs), (W, act_rs),
        (N, out_sh), (N, proj_sh), (W * N, final),
    ):
        each(count, make, "wait_send")


def per_device(
    cand_acts, cand_grads, query_acts, query_grads, basis_in, basis_out, eigvals, slot_pair
):
    W = lax.axis_size("wide")
    N = lax.axis_size("narrow")
    T, F = cand_acts.shape
    D = cand_grads.shape[1]
    Q = query_acts.shape[0]
    KA = basis_in.shape[1]
    G, J = eigvals.shape
    QN = Q // N
    TW, QW = T // W, QN // W
    PR = PAIRS // (W * N)
    queries = Q // QPER
    qpad = -(-queries // 128) * 128
    C = next(c for c in range(max(F // 1024, 1), F + 1) if F % (c * 128) == 0)
    CK = F // C
    GT = 32
    groups = Q // GT
    wire = BF16 if TW % 16 == 0 else F32
    scale = 1.0 / math.sqrt(G * J * W * QPER * TOK_DEV * N / PAIRS)
    vm = pltpu.VMEM
    dma = pltpu.SemaphoreType.DMA
    scratch = [
        vm((G, J), F32), vm((1, T), jnp.int32),
        vm((C, T + QN, CK), BF16), vm((C, CK, KA), BF16), vm((T, D), BF16), vm((QN, D), BF16),
        vm((D, G), BF16), vm((T + QN, KA), F32),
        vm((W, TW, G), F32), vm((W, TW, G), wire), vm((W, TW, G), wire), vm((W, TW, G), wire),
        vm((W, QW, G), F32), vm((W, QW, G), F32), vm((W, QW, G), F32),
        vm((W, QN, J), F32), vm((W, QN, J), F32), vm((W, T, J), BF16), vm((W, T, J), BF16),
        vm((N, QN, G), F32), vm((N, QN, J), F32),
        vm((groups, GT // QPER * J, G), BF16), vm((J, T), F32), vm((T, G), F32), vm((qpad, T), F32),
        vm((W * N, PR, qpad), F32), vm((W * N, PR, qpad), F32),
        dma((5,)), dma((C,)), dma((C,)), dma((C,)),
    ] + [dma((W,))] * 12 + [dma((N,))] * 4 + [dma((W * N,))] * 2
    hbm = pl.BlockSpec(memory_space=pl.ANY)
    vmem = pl.BlockSpec(memory_space=pltpu.VMEM)
    return pl.pallas_call(
        functools.partial(kernel, W, N, scale),
        out_shape=jax.ShapeDtypeStruct((PR, queries), F32),
        in_specs=[hbm] * 8,
        out_specs=vmem,
        scratch_shapes=scratch,
        compiler_params=pltpu.CompilerParams(
            collective_id=0, has_side_effects=True, vmem_limit_bytes=63 * 2**20
        ),
        cost_estimate=pl.CostEstimate(
            flops=2 * (T + QN) * F * KA, bytes_accessed=2 * F * (KA + T + QN), transcendentals=0
        ),
    )(
        cand_acts, cand_grads, query_acts, query_grads, basis_in, basis_out, eigvals,
        slot_pair.reshape(1, T),
    )


def solution(mesh):
    in_specs = (
        P(("groups", "narrow"), "wide"),
        P(("groups", "narrow"), "wide"),
        P("groups", "wide"),
        P("groups", "wide"),
        P("wide", None),
        P("wide", None),
        P(None, "wide"),
        P(("groups", "narrow")),
    )
    out_specs = P(("groups", "wide", "narrow"), None)
    return jax.shard_map(
        per_device, mesh=mesh, in_specs=in_specs, out_specs=out_specs, check_vma=False
    )
```

```python
import functools
import math

import jax
import jax.numpy as jnp
from jax import lax
from jax.experimental import pallas as pl
from jax.experimental.pallas import tpu as pltpu
from jax.sharding import PartitionSpec as P

QPER = 4
TOK_DEV = 128
PAIRS = 128
MESH = pl.DeviceIdType.MESH
F32 = jnp.float32
BF16 = jnp.bfloat16


def nt_dot(a, b, precision=None):
    return lax.dot_general(
        a, b, (((1,), (1,)), ((), ())), precision=precision, preferred_element_type=F32
    )


def tn_dot(a, b):
    return lax.dot_general(a, b, (((0,), (0,)), ((), ())), preferred_element_type=F32)


def kernel(
    W, N, scale,
    ca, cg, qa, qg, bi, bo, eig_hbm, sp_hbm,
    out,
    eig, sp, x, vbi, vcg, vqg, vbo, acc,
    g_own, g_send, g_recv, g_all,
    o_send, o_recv, o_all,
    p_send, p_recv, a_send, a_recv,
    qo_all, qp_all,
    table, act_t, grad, tsc,
    f_send, f_recv,
    ld_sem, bi_sem, ca_sem, qa_sem,
    gs_s, gs_r, ga_s, ga_r, os_s, os_r, oa_s, oa_r,
    ps_s, ps_r, as_s, as_r, no_s, no_r, np_s, np_r, f_s, f_r,
):
    w = lax.axis_index("wide")
    n = lax.axis_index("narrow")
    me = w * N + n
    C, rows, CK = x.shape
    T = ca.shape[0]
    QN = rows - T
    G = bo.shape[1]
    J = eig.shape[1]
    TW = g_send.shape[1]
    QW = o_send.shape[1]
    PR = f_send.shape[1]
    queries = N * QN // QPER
    wire = g_send.dtype

    q_rows = pl.ds(pl.multiple_of(n * QN, QN), QN)
    loads = [
        pltpu.make_async_copy(bo, vbo, ld_sem.at[0]),
        pltpu.make_async_copy(qg.at[q_rows], vqg, ld_sem.at[1]),
        pltpu.make_async_copy(cg, vcg, ld_sem.at[2]),
    ]
    late = [
        pltpu.make_async_copy(eig_hbm, eig, ld_sem.at[3]),
        pltpu.make_async_copy(sp_hbm, sp, ld_sem.at[4]),
    ]
    for c in loads:
        c.start()

    def chunk_copies(c):
        cols = pl.ds(c * CK, CK)
        return (
            pltpu.make_async_copy(bi.at[cols], vbi.at[c], bi_sem.at[c]),
            pltpu.make_async_copy(ca.at[:, cols], x.at[c, pl.ds(0, T)], ca_sem.at[c]),
            pltpu.make_async_copy(qa.at[q_rows, cols], x.at[c, pl.ds(T, QN)], qa_sem.at[c]),
        )

    for c in range(C):
        for copy in chunk_copies(c):
            copy.start()
    for c in late:
        c.start()

    barrier = pltpu.get_barrier_semaphore()

    def greet(d, _):
        k = lax.rem(me + d, W * N)
        pl.semaphore_signal(
            barrier, inc=1, device_id={"wide": k // N, "narrow": lax.rem(k, N)},
            device_id_type=MESH,
        )
        return 0

    lax.fori_loop(1, W * N, greet, 0)

    def wide_of(d):
        return lax.rem(w + d, W)

    def scatter(send, recv, s, r, d):
        k = wide_of(d)
        return pltpu.make_async_remote_copy(
            src_ref=send.at[k], dst_ref=recv.at[d], send_sem=s.at[d], recv_sem=r.at[d],
            device_id={"wide": k}, device_id_type=MESH,
        )

    def gather(buf, s, r, d):
        return pltpu.make_async_remote_copy(
            src_ref=buf.at[w], dst_ref=buf.at[w], send_sem=s.at[d], recv_sem=r.at[d],
            device_id={"wide": wide_of(d)}, device_id_type=MESH,
        )

    def share(buf, s, r, d):
        return pltpu.make_async_remote_copy(
            src_ref=buf.at[n], dst_ref=buf.at[n], send_sem=s.at[d], recv_sem=r.at[d],
            device_id={"narrow": lax.rem(n + d, N)}, device_id_type=MESH,
        )

    def final(d):
        k = lax.rem(me + d, W * N)
        return pltpu.make_async_remote_copy(
            src_ref=f_send.at[k], dst_ref=f_recv.at[d], send_sem=f_s.at[d], recv_sem=f_r.at[d],
            device_id={"wide": k // N, "narrow": lax.rem(k, N)}, device_id_type=MESH,
        )

    def each(count, make, what):
        def body(d, _):
            getattr(make(d), what)()
            return 0

        lax.fori_loop(1, count, body, 0)

    grad_rs = functools.partial(scatter, g_send, g_recv, gs_s, gs_r)
    out_rs = functools.partial(scatter, o_send, o_recv, os_s, os_r)
    proj_rs = functools.partial(scatter, p_send, p_recv, ps_s, ps_r)
    act_rs = functools.partial(scatter, a_send, a_recv, as_s, as_r)
    grad_ag = functools.partial(gather, g_all, ga_s, ga_r)
    out_ag = functools.partial(gather, o_all, oa_s, oa_r)
    out_sh = functools.partial(share, qo_all, no_s, no_r)
    proj_sh = functools.partial(share, qp_all, np_s, np_r)

    loads[0].wait()
    loads[1].wait()
    part = jnp.dot(vqg[...], vbo[...], preferred_element_type=F32)
    for k in range(W):
        o_send[k] = part[k * QW : (k + 1) * QW]
    loads[2].wait()
    part = jnp.dot(vcg[...], vbo[...], preferred_element_type=F32)
    for k in range(W):
        block = part[k * TW : (k + 1) * TW]
        g_own[k] = block
        g_send[k] = block.astype(wire)

    def project(c, _):
        cols = pl.ds(c * CK, CK)
        pltpu.make_async_copy(bi.at[cols], vbi.at[c], bi_sem.at[c]).wait()
        pltpu.make_async_copy(ca.at[:, cols], x.at[c, pl.ds(0, T)], ca_sem.at[c]).wait()
        pltpu.make_async_copy(
            qa.at[q_rows, cols], x.at[c, pl.ds(T, QN)], qa_sem.at[c]
        ).wait()
        acc[...] += jnp.dot(x[c], vbi[c], preferred_element_type=F32)
        return 0

    acc[...] = jnp.zeros_like(acc)
    first, mid = 0, C * 6 // 7
    lax.fori_loop(0, first, project, 0)
    pl.semaphore_wait(barrier, W * N - 1)
    each(W, out_rs, "start")
    each(W, grad_rs, "start")
    lax.fori_loop(first, mid, project, 0)

    each(W, out_rs, "wait_recv")
    total = o_send[w]
    for d in range(1, W):
        total = total + o_recv[d]
    o_all[w] = total
    each(W, out_ag, "start")
    lax.fori_loop(mid, C, project, 0)

    for k in range(W):
        p_send[k] = acc[T:, k * J : (k + 1) * J]
    each(W, proj_rs, "start")

    each(W, out_ag, "wait_recv")
    for k in range(W):
        qo_all[n, k * QW : (k + 1) * QW, :] = o_all[k]
    each(N, out_sh, "start")

    each(W, grad_rs, "wait_recv")
    total = g_own[w]
    for d in range(1, W):
        total = total + g_recv[d].astype(F32)
    g_all[w] = total.astype(BF16).astype(wire)
    each(W, grad_ag, "start")
    for k in range(W):
        a_send[k] = acc[:T, k * J : (k + 1) * J].astype(BF16)
    each(W, act_rs, "start")

    for c in late:
        c.wait()
    recip = (1.0 / eig[...]).T
    each(W, proj_rs, "wait_recv")
    total = p_send[w]
    for d in range(1, W):
        total = total + p_recv[d]
    qp_all[n] = total
    each(N, proj_sh, "start")

    groups, GT = table.shape[0], table.shape[1] // J * QPER
    three = 3 * GT
    per = QN // GT
    GQ = GT // QPER
    token = lax.rem(lax.broadcasted_iota(jnp.int32, (three, G), 0), GT)

    def build(step, _):
        d = step // per

        @pl.when((d > 0) & (lax.rem(step, per) == 0))
        def _():
            out_sh(d).wait_recv()
            proj_sh(d).wait_recv()

        at = lax.rem(n + N - d, N)
        lo = pl.multiple_of(lax.rem(step, per) * GT, GT)
        val = qp_all[at, pl.ds(lo, GT), :]
        hi = val.astype(BF16).astype(F32)
        left = jnp.concatenate([hi, hi, val - hi], axis=0).astype(BF16)
        val = qo_all[at, pl.ds(lo, GT), :]
        hi = val.astype(BF16).astype(F32)
        right = jnp.concatenate([hi, val - hi, hi], axis=0)
        g = at * per + lax.rem(step, per)
        for k in range(GQ):
            mine = jnp.where((token >= k * QPER) & (token < (k + 1) * QPER), right, 0.0)
            block = tn_dot(left, mine.astype(BF16)) * recip
            table[g, k * J : (k + 1) * J, :] = block.astype(BF16)
        return 0

    lax.fori_loop(0, groups, build, 0)

    each(W, grad_ag, "wait_recv")
    for k in range(W):
        grad[k * TW : (k + 1) * TW, :] = g_all[k].astype(F32)
    grads = grad[...].astype(BF16)
    tsc[...] = jnp.zeros_like(tsc)
    each(W, act_rs, "wait_recv")
    own = a_send[w].astype(F32)
    for d in range(1, W):
        own = own + a_recv[d].astype(F32)
    act_t[...] = own.T

    def score(g, _):
        h = nt_dot(table[g], grads)
        for k in range(GQ):
            rowsum = jnp.sum(h[k * J : (k + 1) * J] * act_t[...], axis=0, keepdims=True)
            tsc[pl.ds(g * GQ + k, 1), :] = rowsum
        return 0

    lax.fori_loop(0, groups, score, 0)

    pair = lax.broadcasted_iota(jnp.int32, (PAIRS, T), 0)
    onehot = (pair == sp[...]).astype(F32)
    value = nt_dot(onehot, tsc[...], lax.Precision.HIGHEST)
    for k in range(W * N):
        f_send[k] = value[k * PR : (k + 1) * PR]
    each(W * N, final, "start")
    each(W * N, final, "wait_recv")
    total = f_send[me]
    for d in range(1, W * N):
        total = total + f_recv[d]
    out[...] = total[:, :queries] * scale

    for count, make in (
        (W, out_rs), (W, grad_rs), (W, out_ag), (W, grad_ag), (W, proj_rs), (W, act_rs),
        (N, out_sh), (N, proj_sh), (W * N, final),
    ):
        each(count, make, "wait_send")


def per_device(
    cand_acts, cand_grads, query_acts, query_grads, basis_in, basis_out, eigvals, slot_pair
):
    W = lax.axis_size("wide")
    N = lax.axis_size("narrow")
    T, F = cand_acts.shape
    D = cand_grads.shape[1]
    Q = query_acts.shape[0]
    KA = basis_in.shape[1]
    G, J = eigvals.shape
    QN = Q // N
    TW, QW = T // W, QN // W
    PR = PAIRS // (W * N)
    queries = Q // QPER
    qpad = -(-queries // 128) * 128
    C = next(c for c in range(max(F // 1024, 1), F + 1) if F % (c * 128) == 0)
    CK = F // C
    GT = 32
    groups = Q // GT
    wire = BF16 if TW % 16 == 0 else F32
    scale = 1.0 / math.sqrt(G * J * W * QPER * TOK_DEV * N / PAIRS)
    vm = pltpu.VMEM
    dma = pltpu.SemaphoreType.DMA
    scratch = [
        vm((G, J), F32), vm((1, T), jnp.int32),
        vm((C, T + QN, CK), BF16), vm((C, CK, KA), BF16), vm((T, D), BF16), vm((QN, D), BF16),
        vm((D, G), BF16), vm((T + QN, KA), F32),
        vm((W, TW, G), F32), vm((W, TW, G), wire), vm((W, TW, G), wire), vm((W, TW, G), wire),
        vm((W, QW, G), F32), vm((W, QW, G), F32), vm((W, QW, G), F32),
        vm((W, QN, J), F32), vm((W, QN, J), F32), vm((W, T, J), BF16), vm((W, T, J), BF16),
        vm((N, QN, G), F32), vm((N, QN, J), F32),
        vm((groups, GT // QPER * J, G), BF16), vm((J, T), F32), vm((T, G), F32), vm((qpad, T), F32),
        vm((W * N, PR, qpad), F32), vm((W * N, PR, qpad), F32),
        dma((5,)), dma((C,)), dma((C,)), dma((C,)),
    ] + [dma((W,))] * 12 + [dma((N,))] * 4 + [dma((W * N,))] * 2
    hbm = pl.BlockSpec(memory_space=pl.ANY)
    vmem = pl.BlockSpec(memory_space=pltpu.VMEM)
    return pl.pallas_call(
        functools.partial(kernel, W, N, scale),
        out_shape=jax.ShapeDtypeStruct((PR, queries), F32),
        in_specs=[hbm] * 8,
        out_specs=vmem,
        scratch_shapes=scratch,
        compiler_params=pltpu.CompilerParams(
            collective_id=0, has_side_effects=True, vmem_limit_bytes=63 * 2**20
        ),
        cost_estimate=pl.CostEstimate(
            flops=2 * (T + QN) * F * KA, bytes_accessed=2 * F * (KA + T + QN), transcendentals=0
        ),
    )(
        cand_acts, cand_grads, query_acts, query_grads, basis_in, basis_out, eigvals,
        slot_pair.reshape(1, T),
    )


def solution(mesh):
    in_specs = (
        P(("groups", "narrow"), "wide"),
        P(("groups", "narrow"), "wide"),
        P("groups", "wide"),
        P("groups", "wide"),
        P("wide", None),
        P("wide", None),
        P(None, "wide"),
        P(("groups", "narrow")),
    )
    out_specs = P(("groups", "wide", "narrow"), None)
    return jax.shard_map(
        per_device, mesh=mesh, in_specs=in_specs, out_specs=out_specs, check_vma=False
    )
```
